32 devices in a mesh: groups: 2 (over x), tensor: 16 (over z, y, core).
Axes of the slice: x: 2, y: 2, z: 4, core: 2. Of those that a mesh axis runs over, the one named last changes fastest.
Arguments:
- down_weight: bfloat16 [2, 28672, 6144], P(None, 'tensor'), may hold values from -6 to 6
- generator_left: float32 [32, 128, 128], P(('groups', 'tensor')), parts along dimension 0, may hold values from -0.5 to 0.5
- generator_right: float32 [32, 224, 224], P(('groups', 'tensor')), parts along dimension 0, may hold values from -0.375 to 0.375
- owner_map: int32 [4], P('groups'), parts along dimension 0, may hold values from 0 to 15
Outputs:
- merged: bfloat16 [4, 28672, 6144], P('groups', 'tensor'), parts along dimension 0
The draws below stay inside these ranges and needn't reach their ends.
There are 2 independent parts, one for each index of `groups`. The reference program is written for one: setup_inputs(seed, part) draws one part's arguments, and reference() takes and returns one part's arrays. A program takes and returns all parts, laid end to end along the dimension named above; an argument that names none is the same for every part. Nothing has to cross between parts.
All inputs are finite; a program needn't handle non-finite values.
Results may differ from the reference program's by a relative error of at most 0.0049.
Values may be sent and summed in bfloat16 or wider, within the bound.
A program may use at most 384 MiB of HBM per device.

```python
import jax
import jax.numpy as jnp
from jax import lax

FF = 28672
ORDER_A = 128
ORDER_B = 224
COLS = 6144
LAYERS = 2
N_TENSOR = 16


def block_levels(rng, extent, pieces, low, largest):
    loudness, own = 1.0, jax.random.fold_in(rng, 6)
    for axis_at, shards_of in pieces:
        heights = jnp.exp(jax.random.uniform(jax.random.fold_in(own, axis_at), (shards_of,), jnp.float32, low / len(pieces), largest / len(pieces)))
        loudness = loudness * jnp.repeat(heights, extent[axis_at] // shards_of).reshape([-1 if axis == axis_at else 1 for axis in range(len(extent))])
    return loudness


def gaussian(own_key, shape, scale, reach, cuts=(), kind=jnp.bfloat16):
    array = jax.random.normal(own_key, shape, jnp.float32) * scale
    if len(cuts) > 0:
        array = block_levels(own_key, shape, cuts, -0.22, 0.18) * array
    return jnp.clip(array, min=-reach, max=reach).astype(kind)


def setup_inputs(seed: int = 0, part: int = 0) -> dict:
    keys = jax.random.split(jax.random.key(seed), 5)
    part_keys = jax.random.split(jax.random.fold_in(keys[4], part), 5)
    return {
        "down_weight": gaussian(keys[0], (LAYERS, FF, COLS), 1.0, 6.0, ((1, 16),)),
        "generator_left": gaussian(part_keys[1], (N_TENSOR, ORDER_A, ORDER_A), ORDER_A ** -0.5, 0.5, ((0, 16),), jnp.float32),
        "generator_right": gaussian(part_keys[2], (N_TENSOR, ORDER_B, ORDER_B), ORDER_B ** -0.5, 0.375, ((0, 16),), jnp.float32),
        "owner_map": jax.random.randint(part_keys[3], (LAYERS,), 0, N_TENSOR).astype(jnp.int32),
    }


def cayley(raw):
    skewed = 0.5 * (raw - raw.T)
    identity = jnp.eye(raw.shape[0], dtype=raw.dtype)
    shifted = identity - skewed
    numerator = jnp.dot(shifted, shifted, precision=lax.Precision.HIGHEST)
    gramian = identity - jnp.dot(skewed, skewed, precision=lax.Precision.HIGHEST)
    lower_part = jnp.linalg.cholesky(gramian)
    return jax.scipy.linalg.cho_solve((lower_part, True), numerator)

def reference(down_weight, generator_left, generator_right, owner_map):
    outputs = []
    for layer_index in range(LAYERS):
        holder = owner_map[layer_index]
        factor_left = cayley(generator_left[holder])
        factor_right = cayley(generator_right[holder])
        weights = down_weight[layer_index].reshape(ORDER_A, ORDER_B, COLS).astype(jnp.float32)
        rotated = jnp.einsum('bk,akc->abc', factor_right, weights, precision=lax.Precision.HIGHEST).astype(jnp.bfloat16)
        merged = jnp.dot(factor_left, rotated.reshape(ORDER_A, ORDER_B * COLS).astype(jnp.float32), precision=lax.Precision.HIGHEST)
        outputs.append(merged.astype(jnp.bfloat16).reshape(ORDER_A * ORDER_B, COLS))
    return jnp.stack(outputs)
```

```python
import jax
import jax.numpy as jnp
from jax import lax
from jax.experimental import pallas as pl
from jax.experimental.pallas import tpu as pltpu
from jax.sharding import PartitionSpec as P

CHUNKS = 3


def cayley(raw):
    skewed = 0.5 * (raw - raw.T)
    identity = jnp.eye(raw.shape[0], dtype=raw.dtype)
    shifted = identity - skewed
    numerator = jnp.dot(shifted, shifted, precision=lax.Precision.HIGHEST)
    gramian = identity - jnp.dot(skewed, skewed, precision=lax.Precision.HIGHEST)
    lower_part = jnp.linalg.cholesky(gramian)
    return jax.scipy.linalg.cho_solve((lower_part, True), numerator)


def copy_block(group_ref, source_ref, *refs):
    refs[-1][...] = source_ref[...].reshape(refs[-1].shape)


def pack(down_weight, group, chunk, tensor, width):
    rows = down_weight.shape[1]
    return pl.pallas_call(
        copy_block,
        grid_spec=pltpu.PrefetchScalarGridSpec(
            num_scalar_prefetch=1,
            grid=(tensor,),
            in_specs=[pl.BlockSpec((1, rows, width), lambda t, g: (g[0], 0, chunk * tensor + t))],
            out_specs=pl.BlockSpec((1, rows, width), lambda t, g: (t, 0, 0)),
        ),
        out_shape=jax.ShapeDtypeStruct((tensor, rows, width), down_weight.dtype),
        cost_estimate=pl.CostEstimate(
            flops=0, bytes_accessed=4 * tensor * rows * width, transcendentals=0
        ),
    )(group, down_weight)


def unpack(back, group, merged, chunk, shape):
    layers, tensor, rows, width = back.shape
    more = [] if merged is None else [merged]
    return pl.pallas_call(
        copy_block,
        grid_spec=pltpu.PrefetchScalarGridSpec(
            num_scalar_prefetch=1,
            grid=(layers, tensor),
            in_specs=[pl.BlockSpec((1, 1, rows, width), lambda l, t, g: (l, t, 0, 0))]
            + [pl.BlockSpec(memory_space=pl.ANY) for _ in more],
            out_specs=pl.BlockSpec((1, rows, width), lambda l, t, g: (l, 0, chunk * tensor + t)),
        ),
        out_shape=jax.ShapeDtypeStruct(shape, back.dtype),
        input_output_aliases={2: 0} if more else {},
        cost_estimate=pl.CostEstimate(
            flops=0, bytes_accessed=4 * layers * tensor * rows * width, transcendentals=0
        ),
    )(group, back, *more)


def body(groups, tensor, down_weight, generator_left, generator_right, owner_map):
    layers, rows, columns = down_weight.shape
    order_left = generator_left.shape[1]
    order_right = generator_right.shape[1]
    rows_left = rows // order_right
    own_columns = columns // tensor
    aligned = own_columns % (CHUNKS * 128) == 0
    chunks = CHUNKS if aligned else 1
    width = own_columns // chunks
    group = lax.axis_index("groups")
    me = lax.axis_index("tensor")
    which = group.reshape(1).astype(jnp.int32)

    def outgoing(chunk):
        if aligned:
            return pack(down_weight, which, chunk, tensor, width)
        weights = lax.dynamic_index_in_dim(down_weight, group, 0, keepdims=False)
        return weights.reshape(rows, tensor, width).transpose(1, 0, 2)

    def forward(send):
        block = lax.all_to_all(send, "tensor", 0, 0, tiled=True)
        return block.reshape(order_left, order_right, width)

    tie = lax.optimization_barrier
    first, raw_left, raw_right = tie((outgoing(0), generator_left[0], generator_right[0]))
    received = [forward(first)]
    own_left = cayley(raw_left)
    own_right = cayley(raw_right)
    if chunks > 1:
        send, received[0], own_left, own_right = tie(
            (outgoing(1), received[0], own_left, own_right)
        )
        received.append(forward(send))

    mine = owner_map == me
    left = jnp.where(mine[:, None, None], own_left, 0.0)
    right = jnp.where(mine[:, None, None], own_right, 0.0)
    left, right = lax.psum((left, right), "tensor")
    for chunk in range(2, chunks):
        send, received[-1], left, right = tie((outgoing(chunk), received[-1], left, right))
        received.append(forward(send))
    left = lax.all_to_all(left, "groups", 0, 0, tiled=True)
    right = lax.all_to_all(right, "groups", 0, 0, tiled=True)

    def place(back, merged, chunk):
        if aligned:
            return unpack(back, which, merged, chunk, down_weight.shape)
        return back.transpose(0, 2, 1, 3).reshape(layers, rows, columns)

    merged = None
    for chunk in range(chunks):
        block = received[chunk].astype(jnp.float32)
        outputs = []
        for target in range(groups):
            rotated = jnp.einsum(
                "bk,akc->abc", right[target], block, precision=lax.Precision.HIGHEST
            ).astype(jnp.bfloat16)
            product = jnp.einsum(
                "ak,kbc->abc", left[target], rotated.astype(jnp.float32), precision=lax.Precision.HIGHEST
            ).astype(jnp.bfloat16)
            outputs.append(product.reshape(tensor, rows, width))
        send = jnp.concatenate(outputs, axis=0)
        if chunk == 0:
            send, received[-1] = tie((send, received[-1]))
        else:
            send, back = tie((send, back))
            merged = place(back, merged, chunk - 1)
        back = lax.all_to_all(send, ("groups", "tensor"), 0, 0, tiled=True)
        back = back.reshape(groups, tensor, rows, width)
    return place(back, merged, chunks - 1)


def solution(mesh):
    groups, tensor = mesh.shape["groups"], mesh.shape["tensor"]
    placed = (
        P(None, "tensor", None),
        P(("groups", "tensor"), None, None),
        P(("groups", "tensor"), None, None),
        P("groups"),
    )

    def step(*arrays):
        return body(groups, tensor, *arrays)

    return jax.shard_map(
        step, mesh=mesh, in_specs=placed, out_specs=P("groups", "tensor", None), check_vma=False
    )
```
